256 devices in a mesh: col: 8 (over y, x_hi), sec: 32 (over x_lo, z, core).
Axes of the slice: x: 4 (x_hi: 2, x_lo: 2; x = x_hi * 2 + x_lo), y: 4, z: 8, core: 2. Of those that a mesh axis runs over, the one named last changes fastest.
Arguments:
- corner: bfloat16 [8, 64, 4096], P('col', 'sec'), may hold values from -6 to 6
- edge: bfloat16 [8, 256, 64, 4096], P('col', 'sec'), may hold values from -0.75 to 0.75
- closing: bfloat16 [8, 256, 64, 4096], P('col', 'sec'), may hold values from -0.09375 to 0.09375
- projector: float32 [8, 64, 4096], P('col', 'sec'), may hold values from -0.75 to 0.75
- left_slot: int32 [8, 256], P('col', 'sec'), may hold values from 0 to 1
- out_sector: int32 [8, 256], P('col', 'sec'), may hold values from 0 to 63
- owner: int32 [64], replicated, may hold values from 0 to 31, as said below
Outputs:
- new_corner: float32 [8, 64, 4096], P('col', 'sec')
The draws below stay inside these ranges and needn't reach their ends.
Inputs may be any that keep to these rules, and one draw needn't show every extreme that they name: `owner`: every index of sec owns exactly 2 sectors.
All inputs are finite; a program needn't handle non-finite values. Where the reference program divides by a largest or mean magnitude, that divisor is 1e-20 or more.
Results may differ from the reference program's by a relative error of at most 0.0031.
Values sent between devices are 32-bit elements; how exact they have to be, the bound alone decides.
No kernel may reach another device: no remote copies, remote signals or barrier semaphores. Data moves between devices by JAX's collectives and lax.ppermute only.
A program may use at most 64 MiB of HBM per device.

```python
import math
import jax
import jax.numpy as jnp
import numpy as np
from jax import lax

B = 64
WIDE = 4096
SEC_DEV = 2
PAIR_DEV = 8
SECTORS = 64
PAIRS = 256
COLUMNS = 8
N_SEC = 32


def draw_owner(key, part):
    key = jax.random.fold_in(key, 1)
    base = jnp.arange(SEC_DEV * N_SEC, dtype=jnp.int32) % N_SEC
    return jax.random.permutation(key, base).astype(jnp.int32)


def place_ends(array, own_key, low, high):
    spot = [jax.random.randint(jax.random.fold_in(own_key, axis), (), 0, length) for axis, length in enumerate(array.shape)]
    widest = array.shape.index(max(array.shape))
    beside = spot[:widest] + [(spot[widest] + 1) % array.shape[widest]] + spot[widest + 1:]
    return array.at[tuple(spot)].set(low).at[tuple(beside)].set(high)


def levels(own_key, shape, pieces, low, largest):
    def one(position, shards_of):
        heights = jax.random.uniform(jax.random.fold_in(jax.random.fold_in(own_key, 6), position), (shards_of,), jnp.float32, low / len(pieces), largest / len(pieces))
        return jnp.repeat(jnp.exp(heights), shape[position] // shards_of).reshape((-1,) + (1,) * (len(shape) - position - 1))

    loudness = one(*pieces[0])
    for cut in pieces[1:]:
        loudness = loudness * one(*cut)
    return loudness


def rank_bounds(count, lean):
    loads = [(1 << 20) // math.isqrt(standing ** lean) + 1 for standing in range(1, count + 1)]
    deviation = 1 + sum(loads) // (1 << 30)
    return np.cumsum(np.array([max(1, weight // deviation) for weight in loads]))


def skewed_ids(stream_key, shape, number_of, slope):
    table = rank_bounds(number_of, slope)
    pick = jax.random.randint(jax.random.fold_in(stream_key, 1), shape, 0, int(table[number_of - 1]))
    standing = jnp.searchsorted(jnp.asarray(table, jnp.int32), pick, side="right")
    return jax.random.permutation(jax.random.fold_in(stream_key, 2), number_of)[standing].astype(jnp.int32)


def gaussian(stream_key, extent, spread, reach, shards=(), kind=jnp.bfloat16):
    drawn = jax.random.normal(stream_key, extent, jnp.float32) * spread
    if len(shards) > 0:
        drawn = levels(stream_key, extent, shards, -0.22, 0.18) * drawn
    return jnp.clip(drawn, min=-reach, max=reach).astype(kind)


def setup_inputs(seed: int = 0) -> dict:
    key_of = jax.random.split(jax.random.key(seed), 8)
    return {
        "corner": gaussian(key_of[0], (COLUMNS, SECTORS, B * B), 1.0, 6.0, ((0, 8), (1, 32))),
        "edge": gaussian(key_of[1], (COLUMNS, PAIRS, B, WIDE), B ** -0.5, 0.75, ((0, 8), (1, 32))),
        "closing": gaussian(key_of[2], (COLUMNS, PAIRS, B, WIDE), WIDE ** -0.5, 0.09375, ((0, 8), (1, 32))),
        "projector": gaussian(key_of[3], (COLUMNS, SECTORS, B * B), B ** -0.5, 0.75, ((0, 8), (1, 32)), jnp.float32),
        "left_slot": place_ends(jax.random.randint(key_of[4], (COLUMNS, PAIRS), 0, SEC_DEV), jax.random.fold_in(key_of[4], 1), 0, SEC_DEV - 1).astype(jnp.int32),
        "out_sector": place_ends(skewed_ids(key_of[5], (COLUMNS, PAIRS), SECTORS, 2), jax.random.fold_in(key_of[5], 3), 0, SECTORS - 1).astype(jnp.int32),
        "owner": draw_owner(jax.random.fold_in(key_of[7], 71), 0),
    }


def group_product(items):
    picked, edge, closing = items
    enlarged = jnp.einsum("kab,kbw->kaw", picked.astype(jnp.float32), edge.astype(jnp.float32)).astype(jnp.bfloat16)
    return jnp.einsum("kaw,kcw->kac", enlarged.astype(jnp.float32), closing.astype(jnp.float32))


def one_column(items):
    corner, edge, closing, projector, left_slot, out_sector, order = items
    pairs = edge.shape[0]
    sectors = corner.shape[0]
    groups = pairs // PAIR_DEV
    corner = corner.reshape(sectors, B, B)
    projector = projector.reshape(sectors, B, B)
    chosen = (jnp.arange(pairs, dtype=jnp.int32) // PAIR_DEV) * SEC_DEV + left_slot
    picked = corner[chosen]
    product = lax.map(group_product, (picked.reshape(groups, PAIR_DEV, B, B), edge.reshape(groups, PAIR_DEV, B, WIDE), closing.reshape(groups, PAIR_DEV, B, WIDE)))
    product = product.reshape(pairs, B, B)
    joined = jax.ops.segment_sum(product, out_sector, sectors)[order]
    inner = jnp.einsum("sba,sbc->sac", projector, joined, precision=lax.Precision.HIGHEST)
    projected = jnp.einsum("sac,scd->sad", inner, projector, precision=lax.Precision.HIGHEST)
    scale = jnp.max(jnp.abs(projected)) + 1e-6
    return (projected / scale).reshape(sectors, B * B)


def reference(corner, edge, closing, projector, left_slot, out_sector, owner):
    order = jnp.argsort(owner, stable=True).astype(jnp.int32)
    orders = jnp.broadcast_to(order, (corner.shape[0], order.shape[0]))
    result = lax.map(one_column, (corner, edge, closing, projector, left_slot, out_sector, orders))
    return jnp.roll(result, 1, axis=0)
```

```python
import jax
import jax.numpy as jnp
from jax import lax
from jax.experimental import pallas as pl
from jax.experimental.pallas import tpu as pltpu
from jax.sharding import Mesh, PartitionSpec as P

B = 64
WIDE = 4096
PAIRS = 8
GROUP = 4
TILES = PAIRS // 2
CHUNK = 1024
CHUNKS = WIDE // CHUNK
ROWS = GROUP * B
MSG = TILES * B
SWAP = [(0, 1), (1, 0)]


def low_lanes(shape):
    return lax.broadcasted_iota(jnp.int32, shape, len(shape) - 1) < B


def products_kernel(left_ref, out_ref, owner_ref, corner_ref, edge_ref, closing_ref, msg_ref, edge_buf, closing_buf, lhs_ref, first_ref, edge_sem, closing_sem):
    copies = []
    for g in range(PAIRS // GROUP):
        for w in range(CHUNKS):
            at = (pl.ds(g * ROWS, ROWS), pl.ds(w * CHUNK, CHUNK))
            pair = (
                pltpu.make_async_copy(edge_ref.at[at], edge_buf.at[at], edge_sem.at[g, w]),
                pltpu.make_async_copy(closing_ref.at[at], closing_buf.at[at], closing_sem.at[g, w]),
            )
            pair[0].start()
            pair[1].start()
            copies.append(pair)

    sectors = 2 * 32
    for s in range(sectors - 1, -1, -1):
        first_ref[owner_ref[s]] = s
    slots = []
    for k in range(PAIRS):
        sector = out_ref[k]
        own = owner_ref[sector]
        slots.append((2 * own + jnp.where(first_ref[own] == sector, 0, 1)).astype(jnp.float32))
    low_row = low_lanes((1, 2 * B))
    for t in range(TILES):
        a, b = slots[2 * t], slots[2 * t + 1]
        msg_ref[pl.ds(MSG + 2 * t, 1), :] = jnp.where(low_row, a, b)
        msg_ref[pl.ds(MSG + 2 * t + 1, 1), :] = jnp.where(low_row, b, a)

    low = low_lanes((B, 2 * B))
    lhs_ref[...] = jnp.zeros_like(lhs_ref)
    for k in range(PAIRS):
        i = k % GROUP
        block = corner_ref[left_ref[k]].astype(jnp.float32)
        both = jnp.concatenate([block, block], axis=1)
        mine = jnp.where(low if i % 2 == 0 else ~low, both, 0.0).astype(jnp.bfloat16)
        lhs_ref[pl.ds(k * B, B), pl.ds((i // 2) * 2 * B, 2 * B)] = mine

    for g in range(PAIRS // GROUP):
        total = None
        for w in range(CHUNKS):
            pair = copies[g * CHUNKS + w]
            at = (pl.ds(g * ROWS, ROWS), pl.ds(w * CHUNK, CHUNK))
            pair[0].wait()
            enlarged = jnp.dot(lhs_ref[pl.ds(g * ROWS, ROWS), :], edge_buf[at], preferred_element_type=jnp.float32).astype(jnp.bfloat16)
            pair[1].wait()
            part = lax.dot_general(enlarged, closing_buf[at], (((1,), (1,)), ((), ())), preferred_element_type=jnp.float32)
            total = part if total is None else total + part
        for h in range(GROUP // 2):
            lanes = slice(h * 2 * B, (h + 1) * 2 * B)
            top = total[2 * h * B : (2 * h + 1) * B, lanes]
            bottom = total[(2 * h + 1) * B : (2 * h + 2) * B, lanes]
            msg_ref[pl.ds((g * GROUP // 2 + h) * B, B), :] = jnp.where(low, top, bottom)


def place_kernel(own_ref, other_ref, out_ref, turned_ref):
    dests = out_ref.shape[0]
    core = lax.axis_index("core")
    refs = (own_ref, other_ref)
    for i, ref in enumerate(refs):
        for t in range(TILES):
            turned_ref[i, t] = pltpu.roll(ref[pl.ds(t * B, B), :], B, 1)
    half = jnp.where(low_lanes((1, 2 * B)), 0, 1)
    for d in range(dests):
        slot = (4 * d + 2 * core + half).astype(jnp.float32)
        total = jnp.zeros((B, 2 * B), jnp.float32)
        for i, ref in enumerate(refs):
            for t in range(TILES):
                straight = ref[pl.ds(MSG + 2 * t, 1), :] == slot
                crossed = ref[pl.ds(MSG + 2 * t + 1, 1), :] == slot
                total = total + jnp.where(straight, ref[pl.ds(t * B, B), :], 0.0)
                total = total + jnp.where(crossed, turned_ref[i, t], 0.0)
        out_ref[d] = total


def project_kernel(parts_ref, projector_ref, out_ref, top_ref):
    joined = parts_ref[0]
    for i in range(1, parts_ref.shape[0]):
        joined = joined + parts_ref[i]
    low = low_lanes((B, 2 * B))
    beside = jnp.concatenate([projector_ref[0], projector_ref[1]], axis=1)

    def diagonal(packed):
        return jnp.concatenate([jnp.where(low, packed, 0.0), jnp.where(low, 0.0, packed)], axis=0)

    proj = diagonal(beside)
    inner = jnp.dot(diagonal(joined), proj, precision=lax.Precision.HIGHEST, preferred_element_type=jnp.float32)
    full = lax.dot_general(proj, inner, (((0,), (0,)), ((), ())), precision=lax.Precision.HIGHEST, preferred_element_type=jnp.float32)
    packed = jnp.where(low, full[:B], full[B:])
    out_ref[...] = packed
    size = jnp.abs(packed)
    top = size[:8]
    for i in range(1, 8):
        top = jnp.maximum(top, size[8 * i : 8 * i + 8])
    top_ref[...] = top


VMEM = pl.BlockSpec(memory_space=pltpu.VMEM)
SMEM = pl.BlockSpec(memory_space=pltpu.SMEM)
ANY = pl.BlockSpec(memory_space=pl.ANY)
F32 = jnp.float32


def local(corner, edge, closing, projector, left_slot, out_sector, owner):
    corner = corner.reshape(2, B, B)
    projector = projector.reshape(2, B, B)
    message = pl.pallas_call(
        products_kernel,
        out_shape=jax.ShapeDtypeStruct((MSG + 8, 2 * B), F32),
        in_specs=[SMEM, SMEM, SMEM, VMEM, ANY, ANY],
        out_specs=VMEM,
        scratch_shapes=[
            pltpu.VMEM((PAIRS * B, WIDE), jnp.bfloat16),
            pltpu.VMEM((PAIRS * B, WIDE), jnp.bfloat16),
            pltpu.VMEM((PAIRS * B, ROWS), jnp.bfloat16),
            pltpu.SMEM((32,), jnp.int32),
            pltpu.SemaphoreType.DMA((PAIRS // GROUP, CHUNKS)),
            pltpu.SemaphoreType.DMA((PAIRS // GROUP, CHUNKS)),
        ],
        compiler_params=pltpu.CompilerParams(vmem_limit_bytes=24 << 20),
        name="products",
    )(left_slot[0], out_sector[0], owner, corner, edge.reshape(PAIRS * B, WIDE), closing.reshape(PAIRS * B, WIDE))
    other = lax.ppermute(message, "core", SWAP)
    placed = pl.pallas_call(
        place_kernel,
        out_shape=jax.ShapeDtypeStruct((16, B, 2 * B), F32),
        in_specs=[VMEM, VMEM],
        out_specs=VMEM,
        scratch_shapes=[pltpu.VMEM((2, TILES, B, 2 * B), F32)],
        name="place",
    )(message, other)
    parts = lax.all_to_all(placed, ("xl", "z"), 0, 0)
    packed, top = pl.pallas_call(
        project_kernel,
        out_shape=(jax.ShapeDtypeStruct((B, 2 * B), F32), jax.ShapeDtypeStruct((8, 2 * B), F32)),
        in_specs=[VMEM, VMEM],
        out_specs=(VMEM, VMEM),
        name="project",
    )(parts, projector)
    ahead = [(i, (i + 1) % 8) for i in range(8)]
    blocks = packed.reshape(B, 2, B).transpose(1, 0, 2).reshape(2, B * B)
    moved = lax.ppermute(blocks, "col", ahead)
    top = jnp.maximum(top, lax.ppermute(top, "core", SWAP))
    top = lax.ppermute(top, "col", ahead)
    tops = lax.all_to_all(jnp.broadcast_to(top[None], (16, 8, 2 * B)), ("xl", "z"), 0, 0)
    return (moved / (jnp.max(tops) + 1e-06))[None]


def solution(mesh):
    fine = Mesh(mesh.devices.reshape(8, 2, 8, 2), ("col", "xl", "z", "core"))
    sec = ("xl", "z", "core")
    in_specs = (
        P("col", sec, None),
        P("col", sec, None, None),
        P("col", sec, None, None),
        P("col", sec, None),
        P("col", sec),
        P("col", sec),
        P(),
    )
    return jax.shard_map(local, mesh=fine, in_specs=in_specs, out_specs=P("col", sec, None), check_vma=False)
```

```python
import jax
import jax.numpy as jnp
from jax import lax
from jax.experimental import pallas as pl
from jax.experimental.pallas import tpu as pltpu
from jax.sharding import Mesh, PartitionSpec as P

B = 64
WIDE = 4096
PAIRS = 8
TILES = PAIRS // 2
MSG = TILES * B
SECTORS = 64
ZS = 8
AHEAD = 3
SWAP = [(0, 1), (1, 0)]
F32 = jnp.float32
BF16 = jnp.bfloat16


def low_lanes(shape):
    return lax.broadcasted_iota(jnp.int32, shape, len(shape) - 1) < B


def products_kernel(left_hbm, out_hbm, owner_hbm, corner_hbm, edge_hbm, closing_hbm, msg_ref, left_ref, out_ref, owner_ref, first_ref, corner_ref, rows_ref, both_ref, edge_ref, closing_ref, small_sem, edge_sem, closing_sem):
    small = [
        pltpu.make_async_copy(src, dst, small_sem.at[i])
        for i, (src, dst) in enumerate(((corner_hbm, corner_ref), (left_hbm, left_ref), (owner_hbm, owner_ref), (out_hbm, out_ref)))
    ]
    for copy in small:
        copy.start()
    big = []
    for t in range(TILES):
        rows = pl.ds(t * 2 * B, 2 * B)
        big.append((
            pltpu.make_async_copy(edge_hbm.at[rows], edge_ref.at[rows], edge_sem.at[t]),
            pltpu.make_async_copy(closing_hbm.at[rows], closing_ref.at[rows], closing_sem.at[t]),
        ))
    for t in range(AHEAD):
        big[t][0].start()
        big[t][1].start()

    low = low_lanes((B, 2 * B))
    small[0].wait()
    for r in range(2):
        for t in range(B // 2):
            rows_ref[r, pl.ds(t, 1), :] = corner_ref[pl.ds(r, 1), pl.ds(t * 2 * B, 2 * B)].astype(F32)
    low_half = low_lanes((B // 2, 2 * B))
    for r in range(2):
        packed = rows_ref[r]
        turned = pltpu.roll(packed, B, 1)
        both_ref[r, pl.ds(0, B // 2, stride=2), :] = jnp.where(low_half, packed, turned)
        both_ref[r, pl.ds(1, B // 2, stride=2), :] = jnp.where(low_half, turned, packed)
    small[1].wait()
    lefts = []
    for t in range(TILES):
        top = jnp.where(low, both_ref[left_ref[0, 2 * t]], 0.0)
        bottom = jnp.where(low, 0.0, both_ref[left_ref[0, 2 * t + 1]])
        lefts.append(jnp.concatenate([top, bottom], axis=0).astype(BF16))

    small[2].wait()
    for s in range(SECTORS - 1, -1, -1):
        first_ref[owner_ref[s]] = s
    small[3].wait()
    for k in range(PAIRS):
        sector = out_ref[0, k]
        own = owner_ref[sector]
        slot = (2 * own + jnp.where(first_ref[own] == sector, 0, 1)).astype(F32)
        msg_ref[pl.ds(MSG + k, 1), :] = jnp.full((1, 2 * B), slot, F32)

    for t in range(TILES):
        rows = pl.ds(t * 2 * B, 2 * B)
        big[t][0].wait()
        big[t][1].wait()
        if t + AHEAD < TILES:
            big[t + AHEAD][0].start()
            big[t + AHEAD][1].start()
        enlarged = jnp.dot(lefts[t], edge_ref[rows], preferred_element_type=F32).astype(BF16)
        total = lax.dot_general(enlarged, closing_ref[rows], (((1,), (1,)), ((), ())), preferred_element_type=F32)
        msg_ref[pl.ds(t * B, B), :] = jnp.where(low, total[:B], total[B:])


def place_kernel(m0_ref, m1_ref, m2_ref, m3_ref, out_ref, slots_ref, sem):
    refs = (m0_ref, m1_ref, m2_ref, m3_ref)
    copies = [pltpu.make_async_copy(ref.at[pl.ds(MSG, PAIRS)], slots_ref.at[i], sem.at[i]) for i, ref in enumerate(refs)]
    for copy in copies:
        copy.start()
    core, xl = lax.axis_index("core"), lax.axis_index("xl")
    out_ref[...] = jnp.zeros_like(out_ref)
    low = low_lanes((B, 2 * B))
    half = jnp.where(low, 0, 1)
    for copy in copies:
        copy.wait()
    for i, ref in enumerate(refs):
        for k in range(PAIRS):
            slot = slots_ref[i, k, 0].astype(jnp.int32)
            sec = slot >> 1

            @pl.when(((sec & 1) == core) & ((sec >> 4) == xl))
            def _(ref=ref, k=k, slot=slot, sec=sec):
                tile = ref[pl.ds(k // 2 * B, B), :]
                alone = jnp.where(low, tile, 0.0) if k % 2 == 0 else jnp.where(low, 0.0, tile)
                spread = alone + pltpu.roll(alone, B, 1)
                z = (sec >> 1) & (ZS - 1)
                out_ref[z] = out_ref[z] + jnp.where(half == (slot & 1), spread, 0.0)


def project_kernel(parts_ref, projector_ref, out_ref, top_ref):
    joined = parts_ref[0]
    for i in range(1, parts_ref.shape[0]):
        joined = joined + parts_ref[i]
    low = low_lanes((B, 2 * B))
    beside = jnp.concatenate([projector_ref[0], projector_ref[1]], axis=1)

    def diagonal(packed):
        return jnp.concatenate([jnp.where(low, packed, 0.0), jnp.where(low, 0.0, packed)], axis=0)

    proj = diagonal(beside)
    inner = jnp.dot(diagonal(joined), proj, precision=lax.Precision.HIGHEST, preferred_element_type=F32)
    full = lax.dot_general(proj, inner, (((0,), (0,)), ((), ())), precision=lax.Precision.HIGHEST, preferred_element_type=F32)
    packed = jnp.where(low, full[:B], full[B:])
    out_ref[...] = packed
    size = jnp.abs(packed)
    top = size[:8]
    for i in range(1, 8):
        top = jnp.maximum(top, size[8 * i : 8 * i + 8])
    top_ref[...] = top


VMEM = pl.BlockSpec(memory_space=pltpu.VMEM)
ANY = pl.BlockSpec(memory_space=pl.ANY)
SMALL = pltpu.CompilerParams(vmem_limit_bytes=8 << 20)


def local(corner, edge, closing, projector, left_slot, out_sector, owner):
    message = pl.pallas_call(
        products_kernel,
        out_shape=jax.ShapeDtypeStruct((MSG + PAIRS, 2 * B), F32),
        in_specs=[ANY] * 6,
        out_specs=VMEM,
        scratch_shapes=[
            pltpu.SMEM((1, PAIRS), jnp.int32),
            pltpu.SMEM((1, PAIRS), jnp.int32),
            pltpu.SMEM((SECTORS,), jnp.int32),
            pltpu.SMEM((SECTORS // 2,), jnp.int32),
            pltpu.VMEM((2, B * B), BF16),
            pltpu.VMEM((2, B // 2, 2 * B), F32),
            pltpu.VMEM((2, B, 2 * B), F32),
            pltpu.VMEM((PAIRS * B, WIDE), BF16),
            pltpu.VMEM((PAIRS * B, WIDE), BF16),
            pltpu.SemaphoreType.DMA((4,)),
            pltpu.SemaphoreType.DMA((TILES,)),
            pltpu.SemaphoreType.DMA((TILES,)),
        ],
        compiler_params=pltpu.CompilerParams(vmem_limit_bytes=61 << 20),
        name="products",
    )(left_slot, out_sector, owner, corner[0], edge.reshape(PAIRS * B, WIDE), closing.reshape(PAIRS * B, WIDE))
    over = lax.ppermute(message, "xl", SWAP)
    beside = lax.ppermute(message, "core", SWAP)
    across = lax.ppermute(over, "core", SWAP)
    placed = pl.pallas_call(
        place_kernel,
        out_shape=jax.ShapeDtypeStruct((ZS, B, 2 * B), F32),
        in_specs=[VMEM] * 4,
        out_specs=VMEM,
        scratch_shapes=[pltpu.SMEM((4, PAIRS, 2 * B), F32), pltpu.SemaphoreType.DMA((4,))],
        compiler_params=SMALL,
        name="place",
    )(message, beside, over, across)
    parts = lax.all_to_all(placed, "z", 0, 0)
    packed, top = pl.pallas_call(
        project_kernel,
        out_shape=(jax.ShapeDtypeStruct((B, 2 * B), F32), jax.ShapeDtypeStruct((8, 2 * B), F32)),
        in_specs=[VMEM, VMEM],
        out_specs=(VMEM, VMEM),
        compiler_params=SMALL,
        name="project",
    )(parts, projector.reshape(2, B, B))
    ahead = [(i, (i + 1) % 8) for i in range(8)]
    blocks = packed.reshape(B, 2, B).transpose(1, 0, 2).reshape(2, B * B)
    moved = lax.ppermute(blocks, "col", ahead)
    top = jnp.maximum(top, lax.ppermute(top, "core", SWAP))
    top = lax.ppermute(top, "col", ahead)
    tops = lax.all_to_all(jnp.broadcast_to(top[None], (2 * ZS, 8, 2 * B)), ("xl", "z"), 0, 0)
    return (moved / (jnp.max(tops) + 1e-06))[None]


def solution(mesh):
    fine = Mesh(mesh.devices.reshape(8, 2, ZS, 2), ("col", "xl", "z", "core"))
    sec = ("xl", "z", "core")
    in_specs = (
        P("col", sec, None),
        P("col", sec, None, None),
        P("col", sec, None, None),
        P("col", sec, None),
        P("col", sec),
        P("col", sec),
        P(),
    )
    return jax.shard_map(local, mesh=fine, in_specs=in_specs, out_specs=P("col", sec, None), check_vma=False)
```

```python
import jax
import jax.numpy as jnp
from jax import lax
from jax.experimental import pallas as pl
from jax.experimental.pallas import tpu as pltpu
from jax.sharding import Mesh, PartitionSpec as P

B = 64
WIDE = 4096
PAIRS = 8
TILES = PAIRS // 2
MSG = TILES * B
SECTORS = 64
ZS = 8
AHEAD = 3
SWAP = [(0, 1), (1, 0)]
F32 = jnp.float32
BF16 = jnp.bfloat16


def low_lanes(shape):
    return lax.broadcasted_iota(jnp.int32, shape, len(shape) - 1) < B


def products_kernel(left_hbm, out_hbm, owner_hbm, corner_hbm, edge_hbm, closing_hbm, msg_ref, left_ref, out_ref, owner_ref, first_ref, corner_ref, rows_ref, both_ref, edge_ref, closing_ref, small_sem, edge_sem, closing_sem):
    small = [
        pltpu.make_async_copy(src, dst, small_sem.at[i])
        for i, (src, dst) in enumerate(((corner_hbm, corner_ref), (left_hbm, left_ref), (owner_hbm, owner_ref), (out_hbm, out_ref)))
    ]
    for copy in small:
        copy.start()
    big = []
    for t in range(TILES):
        rows = pl.ds(t * 2 * B, 2 * B)
        big.append((
            pltpu.make_async_copy(edge_hbm.at[rows], edge_ref.at[rows], edge_sem.at[t]),
            pltpu.make_async_copy(closing_hbm.at[rows], closing_ref.at[rows], closing_sem.at[t]),
        ))
    for t in range(AHEAD):
        big[t][0].start()
        big[t][1].start()

    low = low_lanes((B, 2 * B))
    small[0].wait()
    for r in range(2):
        for t in range(B // 2):
            rows_ref[r, pl.ds(t, 1), :] = corner_ref[pl.ds(r, 1), pl.ds(t * 2 * B, 2 * B)].astype(F32)
    low_half = low_lanes((B // 2, 2 * B))
    for r in range(2):
        packed = rows_ref[r]
        turned = pltpu.roll(packed, B, 1)
        both_ref[r, pl.ds(0, B // 2, stride=2), :] = jnp.where(low_half, packed, turned)
        both_ref[r, pl.ds(1, B // 2, stride=2), :] = jnp.where(low_half, turned, packed)
    small[1].wait()
    lefts = []
    for t in range(TILES):
        top = jnp.where(low, both_ref[left_ref[0, 2 * t]], 0.0)
        bottom = jnp.where(low, 0.0, both_ref[left_ref[0, 2 * t + 1]])
        lefts.append(jnp.concatenate([top, bottom], axis=0).astype(BF16))

    small[2].wait()
    for s in range(SECTORS - 1, -1, -1):
        first_ref[owner_ref[s]] = s
    small[3].wait()
    slots = []
    for k in range(PAIRS):
        sector = out_ref[0, k]
        own = owner_ref[sector]
        slots.append((2 * own + jnp.where(first_ref[own] == sector, 0, 1)).astype(F32))
    low_row = low_lanes((1, 2 * B))
    for t in range(TILES):
        a, b = slots[2 * t], slots[2 * t + 1]
        msg_ref[pl.ds(MSG + 2 * t, 1), :] = jnp.where(low_row, a, b)
        msg_ref[pl.ds(MSG + 2 * t + 1, 1), :] = jnp.where(low_row, b, a)

    for t in range(TILES):
        rows = pl.ds(t * 2 * B, 2 * B)
        big[t][0].wait()
        big[t][1].wait()
        if t + AHEAD < TILES:
            big[t + AHEAD][0].start()
            big[t + AHEAD][1].start()
        enlarged = jnp.dot(lefts[t], edge_ref[rows], preferred_element_type=F32).astype(BF16)
        total = lax.dot_general(enlarged, closing_ref[rows], (((1,), (1,)), ((), ())), preferred_element_type=F32)
        msg_ref[pl.ds(t * B, B), :] = jnp.where(low, total[:B], total[B:])


def place_kernel(m0_ref, m1_ref, m2_ref, m3_ref, out_ref, turned_ref):
    refs = (m0_ref, m1_ref, m2_ref, m3_ref)
    for i, ref in enumerate(refs):
        for t in range(TILES):
            turned_ref[i, t] = pltpu.roll(ref[pl.ds(t * B, B), :], B, 1)
    first = 2 * lax.axis_index("core") + 4 * ZS * lax.axis_index("xl")
    half = jnp.where(low_lanes((1, 2 * B)), 0, 1)
    for z in range(ZS):
        slot = (first + 4 * z + half).astype(F32)
        total = jnp.zeros((B, 2 * B), F32)
        for i, ref in enumerate(refs):
            for t in range(TILES):
                straight = ref[pl.ds(MSG + 2 * t, 1), :] == slot
                crossed = ref[pl.ds(MSG + 2 * t + 1, 1), :] == slot
                total = total + jnp.where(straight, ref[pl.ds(t * B, B), :], 0.0)
                total = total + jnp.where(crossed, turned_ref[i, t], 0.0)
        out_ref[z] = total


def project_kernel(parts_ref, projector_ref, out_ref, top_ref):
    joined = parts_ref[0]
    for i in range(1, parts_ref.shape[0]):
        joined = joined + parts_ref[i]
    low = low_lanes((B, 2 * B))
    beside = jnp.concatenate([projector_ref[0], projector_ref[1]], axis=1)

    def diagonal(packed):
        return jnp.concatenate([jnp.where(low, packed, 0.0), jnp.where(low, 0.0, packed)], axis=0)

    proj = diagonal(beside)
    inner = jnp.dot(diagonal(joined), proj, precision=lax.Precision.HIGHEST, preferred_element_type=F32)
    full = lax.dot_general(proj, inner, (((0,), (0,)), ((), ())), precision=lax.Precision.HIGHEST, preferred_element_type=F32)
    packed = jnp.where(low, full[:B], full[B:])
    out_ref[...] = packed
    size = jnp.abs(packed)
    top = size[:8]
    for i in range(1, 8):
        top = jnp.maximum(top, size[8 * i : 8 * i + 8])
    top_ref[...] = top


def finish_kernel(moved_ref, tops_ref, out_ref, rows_ref):
    top = tops_ref[0]
    for i in range(1, tops_ref.shape[0]):
        top = jnp.maximum(top, tops_ref[i])
    scale = jnp.max(top) + 1e-06
    low = low_lanes((B // 2, 2 * B))
    even = moved_ref[pl.ds(0, B // 2, stride=2), :] / scale
    odd = moved_ref[pl.ds(1, B // 2, stride=2), :] / scale
    rows_ref[0] = jnp.where(low, even, pltpu.roll(odd, B, 1))
    rows_ref[1] = jnp.where(low, pltpu.roll(even, B, 1), odd)
    for r in range(2):
        for t in range(B // 2):
            out_ref[pl.ds(r, 1), pl.ds(t * 2 * B, 2 * B)] = rows_ref[r, pl.ds(t, 1), :]


VMEM = pl.BlockSpec(memory_space=pltpu.VMEM)
ANY = pl.BlockSpec(memory_space=pl.ANY)
SMALL = pltpu.CompilerParams(vmem_limit_bytes=8 << 20)


def in_hbm(x):
    return pltpu.with_memory_space_constraint(x, pltpu.HBM)


def local(corner, edge, closing, projector, left_slot, out_sector, owner):
    message = pl.pallas_call(
        products_kernel,
        out_shape=pltpu.VMEM((MSG + PAIRS, 2 * B), F32),
        in_specs=[ANY] * 6,
        out_specs=VMEM,
        scratch_shapes=[
            pltpu.SMEM((1, PAIRS), jnp.int32),
            pltpu.SMEM((1, PAIRS), jnp.int32),
            pltpu.SMEM((SECTORS,), jnp.int32),
            pltpu.SMEM((SECTORS // 2,), jnp.int32),
            pltpu.VMEM((2, B * B), BF16),
            pltpu.VMEM((2, B // 2, 2 * B), F32),
            pltpu.VMEM((2, B, 2 * B), F32),
            pltpu.VMEM((PAIRS * B, WIDE), BF16),
            pltpu.VMEM((PAIRS * B, WIDE), BF16),
            pltpu.SemaphoreType.DMA((4,)),
            pltpu.SemaphoreType.DMA((TILES,)),
            pltpu.SemaphoreType.DMA((TILES,)),
        ],
        compiler_params=pltpu.CompilerParams(vmem_limit_bytes=24 << 20),
        name="products",
    )(*map(in_hbm, (left_slot, out_sector, owner, corner[0], edge.reshape(PAIRS * B, WIDE), closing.reshape(PAIRS * B, WIDE))))
    over = lax.ppermute(message, "xl", SWAP)
    beside = lax.ppermute(message, "core", SWAP)
    over, projector = lax.optimization_barrier((over, projector.reshape(2, B, B)))
    across = lax.ppermute(over, "core", SWAP)
    placed = pl.pallas_call(
        place_kernel,
        out_shape=pltpu.VMEM((ZS, B, 2 * B), F32),
        in_specs=[VMEM] * 4,
        out_specs=VMEM,
        scratch_shapes=[pltpu.VMEM((4, TILES, B, 2 * B), F32)],
        compiler_params=SMALL,
        name="place",
    )(message, beside, over, across)
    parts = lax.all_to_all(placed, "z", 0, 0)
    packed, top = pl.pallas_call(
        project_kernel,
        out_shape=(pltpu.VMEM((B, 2 * B), F32), pltpu.VMEM((8, 2 * B), F32)),
        in_specs=[VMEM, VMEM],
        out_specs=(VMEM, VMEM),
        compiler_params=SMALL,
        name="project",
    )(parts, projector)
    top = jnp.maximum(top, lax.ppermute(top, "core", SWAP))
    moved = lax.ppermute(jnp.concatenate([packed, top], axis=0), "col", [(i, (i + 1) % 8) for i in range(8)])
    tops = lax.all_to_all(jnp.broadcast_to(moved[None, B:], (2 * ZS, 8, 2 * B)), ("xl", "z"), 0, 0)
    return pl.pallas_call(
        finish_kernel,
        out_shape=jax.ShapeDtypeStruct((2, B * B), F32),
        in_specs=[VMEM, VMEM],
        out_specs=VMEM,
        scratch_shapes=[pltpu.VMEM((2, B // 2, 2 * B), F32)],
        compiler_params=SMALL,
        name="finish",
    )(moved, tops)[None]


def solution(mesh):
    fine = Mesh(mesh.devices.reshape(8, 2, ZS, 2), ("col", "xl", "z", "core"))
    sec = ("xl", "z", "core")
    in_specs = (
        P("col", sec, None),
        P("col", sec, None, None),
        P("col", sec, None, None),
        P("col", sec, None),
        P("col", sec),
        P("col", sec),
        P(),
    )
    return jax.shard_map(local, mesh=fine, in_specs=in_specs, out_specs=P("col", sec, None), check_vma=False)
```

```python
import jax
import jax.numpy as jnp
from jax import lax
from jax.experimental import pallas as pl
from jax.experimental.pallas import tpu as pltpu
from jax.sharding import Mesh, PartitionSpec as P

B = 64
WIDE = 4096
PAIRS = 8
TILES = PAIRS // 2
MSG = TILES * B
SECTORS = 64
ZS = 8
AHEAD = 3
SWAP = [(0, 1), (1, 0)]
F32 = jnp.float32
BF16 = jnp.bfloat16


def low_lanes(shape):
    return lax.broadcasted_iota(jnp.int32, shape, len(shape) - 1) < B


def products_kernel(left_hbm, out_hbm, owner_hbm, corner_hbm, edge_hbm, closing_hbm, msg_ref, left_ref, out_ref, owner_ref, first_ref, corner_ref, rows_ref, both_ref, edge_ref, closing_ref, small_sem, edge_sem, closing_sem):
    small = [
        pltpu.make_async_copy(src, dst, small_sem.at[i])
        for i, (src, dst) in enumerate(((corner_hbm, corner_ref), (left_hbm, left_ref), (owner_hbm, owner_ref), (out_hbm, out_ref)))
    ]
    for copy in small:
        copy.start()
    big = []
    for t in range(TILES):
        rows = pl.ds(t * 2 * B, 2 * B)
        big.append((
            pltpu.make_async_copy(edge_hbm.at[rows], edge_ref.at[rows], edge_sem.at[t]),
            pltpu.make_async_copy(closing_hbm.at[rows], closing_ref.at[rows], closing_sem.at[t]),
        ))
    for t in range(AHEAD):
        big[t][0].start()
        big[t][1].start()

    low = low_lanes((B, 2 * B))
    small[0].wait()
    for r in range(2):
        for t in range(B // 2):
            rows_ref[r, pl.ds(t, 1), :] = corner_ref[pl.ds(r, 1), pl.ds(t * 2 * B, 2 * B)].astype(F32)
    low_half = low_lanes((B // 2, 2 * B))
    for r in range(2):
        packed = rows_ref[r]
        turned = pltpu.roll(packed, B, 1)
        both_ref[r, pl.ds(0, B // 2, stride=2), :] = jnp.where(low_half, packed, turned)
        both_ref[r, pl.ds(1, B // 2, stride=2), :] = jnp.where(low_half, turned, packed)
    small[1].wait()
    lefts = []
    for t in range(TILES):
        top = jnp.where(low, both_ref[left_ref[0, 2 * t]], 0.0)
        bottom = jnp.where(low, 0.0, both_ref[left_ref[0, 2 * t + 1]])
        lefts.append(jnp.concatenate([top, bottom], axis=0).astype(BF16))

    small[2].wait()
    for s in range(SECTORS - 1, -1, -1):
        first_ref[owner_ref[s]] = s
    small[3].wait()
    slots = []
    for k in range(PAIRS):
        sector = out_ref[0, k]
        own = owner_ref[sector]
        slots.append((2 * own + jnp.where(first_ref[own] == sector, 0, 1)).astype(F32))
    low_row = low_lanes((1, 2 * B))
    for t in range(TILES):
        a, b = slots[2 * t], slots[2 * t + 1]
        msg_ref[pl.ds(MSG + 2 * t, 1), :] = jnp.where(low_row, a, b)
        msg_ref[pl.ds(MSG + 2 * t + 1, 1), :] = jnp.where(low_row, b, a)

    for t in range(TILES):
        rows = pl.ds(t * 2 * B, 2 * B)
        big[t][0].wait()
        big[t][1].wait()
        if t + AHEAD < TILES:
            big[t + AHEAD][0].start()
            big[t + AHEAD][1].start()
        enlarged = jnp.dot(lefts[t], edge_ref[rows], preferred_element_type=F32).astype(BF16)
        total = lax.dot_general(enlarged, closing_ref[rows], (((1,), (1,)), ((), ())), preferred_element_type=F32)
        msg_ref[pl.ds(t * B, B), :] = jnp.where(low, total[:B], total[B:])


HOPS = ((4, -3), (3, -2), (1, 2), (0, -1))


def place_kernel(m0_ref, m1_ref, m2_ref, m3_ref, *rest):
    out_refs, turned_ref = rest[:-1], rest[-1]
    refs = (m0_ref, m1_ref, m2_ref, m3_ref)
    for i, ref in enumerate(refs):
        for t in range(TILES):
            turned_ref[i, t] = pltpu.roll(ref[pl.ds(t * B, B), :], B, 1)
    core, z = lax.axis_index("core"), lax.axis_index("z")
    first = 4 * ZS * lax.axis_index("xl") + jnp.where(low_lanes((1, 2 * B)), 0, 1)

    def placed(step, to):
        slot = (first + 4 * ((z + step) & (ZS - 1)) + 2 * to).astype(F32)
        total = jnp.zeros((B, 2 * B), F32)
        for i, ref in enumerate(refs):
            for t in range(TILES):
                straight = ref[pl.ds(MSG + 2 * t, 1), :] == slot
                crossed = ref[pl.ds(MSG + 2 * t + 1, 1), :] == slot
                total = total + jnp.where(straight, ref[pl.ds(t * B, B), :], 0.0)
                total = total + jnp.where(crossed, turned_ref[i, t], 0.0)
        return total

    for out_ref, (even, odd) in zip(out_refs, HOPS):
        step = jnp.where(core == 0, even, odd)
        out_ref[0] = placed(step, core)
        out_ref[1] = placed(step, 1 - core)
    out_refs[-1][...] = placed(0, core)


def gather_kernel(*refs):
    own_ref, out_ref = refs[-2:]
    out_ref[0] = refs[0][0] + refs[1][0] + refs[2][0] + refs[3][0] + own_ref[...]
    out_ref[1] = refs[0][1] + refs[1][1] + refs[2][1] + refs[3][1]


def project_kernel(mine_ref, beside_ref, projector_ref, other_ref, out_ref):
    low = low_lanes((B, 2 * B))

    def diagonal(packed):
        return jnp.concatenate([jnp.where(low, packed, 0.0), jnp.where(low, 0.0, packed)], axis=0)

    def project(joined, ref):
        proj = diagonal(jnp.concatenate([ref[0], ref[1]], axis=1))
        inner = jnp.dot(diagonal(joined), proj, precision=lax.Precision.HIGHEST, preferred_element_type=F32)
        full = lax.dot_general(proj, inner, (((0,), (0,)), ((), ())), precision=lax.Precision.HIGHEST, preferred_element_type=F32)
        return jnp.where(low, full[:B], full[B:])

    packed = project(mine_ref[0] + beside_ref[1], projector_ref)
    other = project(mine_ref[1] + beside_ref[0], other_ref)
    out_ref[pl.ds(0, B), :] = packed
    size = jnp.maximum(jnp.abs(packed), jnp.abs(other))
    top = size[:8]
    for i in range(1, 8):
        top = jnp.maximum(top, size[8 * i : 8 * i + 8])
    out_ref[pl.ds(B, 8), :] = top


def finish_kernel(moved_ref, tops_ref, out_ref, rows_ref):
    top = tops_ref[0]
    for i in range(1, tops_ref.shape[0]):
        top = jnp.maximum(top, tops_ref[i])
    scale = jnp.max(top) + 1e-06
    low = low_lanes((B // 2, 2 * B))
    even = moved_ref[pl.ds(0, B // 2, stride=2), :] / scale
    odd = moved_ref[pl.ds(1, B // 2, stride=2), :] / scale
    rows_ref[0] = jnp.where(low, even, pltpu.roll(odd, B, 1))
    rows_ref[1] = jnp.where(low, pltpu.roll(even, B, 1), odd)
    for r in range(2):
        for t in range(B // 2):
            out_ref[pl.ds(r, 1), pl.ds(t * 2 * B, 2 * B)] = rows_ref[r, pl.ds(t, 1), :]


VMEM = pl.BlockSpec(memory_space=pltpu.VMEM)
ANY = pl.BlockSpec(memory_space=pl.ANY)
SMALL = pltpu.CompilerParams(vmem_limit_bytes=8 << 20)


def in_hbm(x):
    return pltpu.with_memory_space_constraint(x, pltpu.HBM)


def local(corner, edge, closing, projector, left_slot, out_sector, owner):
    message = pl.pallas_call(
        products_kernel,
        out_shape=pltpu.VMEM((MSG + PAIRS, 2 * B), F32),
        in_specs=[ANY] * 6,
        out_specs=VMEM,
        scratch_shapes=[
            pltpu.SMEM((1, PAIRS), jnp.int32),
            pltpu.SMEM((1, PAIRS), jnp.int32),
            pltpu.SMEM((SECTORS,), jnp.int32),
            pltpu.SMEM((SECTORS // 2,), jnp.int32),
            pltpu.VMEM((2, B * B), BF16),
            pltpu.VMEM((2, B // 2, 2 * B), F32),
            pltpu.VMEM((2, B, 2 * B), F32),
            pltpu.VMEM((PAIRS * B, WIDE), BF16),
            pltpu.VMEM((PAIRS * B, WIDE), BF16),
            pltpu.SemaphoreType.DMA((4,)),
            pltpu.SemaphoreType.DMA((TILES,)),
            pltpu.SemaphoreType.DMA((TILES,)),
        ],
        compiler_params=pltpu.CompilerParams(vmem_limit_bytes=24 << 20),
        name="products",
    )(*map(in_hbm, (left_slot, out_sector, owner, corner[0], edge.reshape(PAIRS * B, WIDE), closing.reshape(PAIRS * B, WIDE))))
    over = lax.ppermute(message, "xl", SWAP)
    beside = lax.ppermute(message, "core", SWAP)
    projector = projector.reshape(2, B, B)
    other = lax.ppermute(projector, "core", SWAP)
    over, projector, other = lax.optimization_barrier((over, projector, other))
    across = lax.ppermute(over, "core", SWAP)
    tile, both = pltpu.VMEM((B, 2 * B), F32), pltpu.VMEM((2, B, 2 * B), F32)
    *sent, own = pl.pallas_call(
        place_kernel,
        out_shape=[both] * len(HOPS) + [tile],
        in_specs=[VMEM] * 4,
        out_specs=[VMEM] * (len(HOPS) + 1),
        scratch_shapes=[pltpu.VMEM((4, TILES, B, 2 * B), F32)],
        compiler_params=SMALL,
        name="place",
    )(message, beside, over, across)

    def along(x, steps):
        moves = [(2 * z + q, 2 * ((z + steps[q]) % ZS) + q) for z in range(ZS) for q in range(2) if steps[q]]
        return lax.ppermute(x, ("z", "core"), moves)

    came = [along(x, steps) for x, steps in zip(sent, HOPS)]
    mine = pl.pallas_call(gather_kernel, out_shape=both, in_specs=[VMEM] * (len(HOPS) + 1), out_specs=VMEM, compiler_params=SMALL, name="gather")(*came, own)
    beside = lax.ppermute(mine, "core", SWAP)
    payload = pl.pallas_call(
        project_kernel,
        out_shape=pltpu.VMEM((B + 8, 2 * B), F32),
        in_specs=[VMEM] * 4,
        out_specs=VMEM,
        compiler_params=SMALL,
        name="project",
    )(mine, beside, projector, other)
    moved = lax.ppermute(payload, "col", [(i, (i + 1) % 8) for i in range(8)])
    tops = lax.all_to_all(jnp.broadcast_to(moved[None, B:], (2 * ZS, 8, 2 * B)), ("xl", "z"), 0, 0)
    return pl.pallas_call(
        finish_kernel,
        out_shape=jax.ShapeDtypeStruct((2, B * B), F32),
        in_specs=[VMEM, VMEM],
        out_specs=VMEM,
        scratch_shapes=[pltpu.VMEM((2, B // 2, 2 * B), F32)],
        compiler_params=SMALL,
        name="finish",
    )(moved, tops)[None]


def solution(mesh):
    fine = Mesh(mesh.devices.reshape(8, 2, ZS, 2), ("col", "xl", "z", "core"))
    sec = ("xl", "z", "core")
    in_specs = (
        P("col", sec, None),
        P("col", sec, None, None),
        P("col", sec, None, None),
        P("col", sec, None),
        P("col", sec),
        P("col", sec),
        P(),
    )
    return jax.shard_map(local, mesh=fine, in_specs=in_specs, out_specs=P("col", sec, None), check_vma=False)
```

```python
import functools

import jax
import jax.numpy as jnp
from jax import lax
from jax.experimental import pallas as pl
from jax.experimental.pallas import tpu as pltpu
from jax.sharding import Mesh, PartitionSpec as P

B = 64
WIDE = 4096
PAIRS = 8
TILES = PAIRS // 2
MSG = TILES * B
SECTORS = 64
ZS = 8
AHEAD = 3
SWAP = [(0, 1), (1, 0)]
F32 = jnp.float32
BF16 = jnp.bfloat16


def low_lanes(shape):
    return lax.broadcasted_iota(jnp.int32, shape, len(shape) - 1) < B


def products_kernel(left_hbm, out_hbm, owner_hbm, corner_hbm, edge_hbm, closing_hbm, msg_ref, left_ref, out_ref, owner_ref, first_ref, corner_ref, rows_ref, both_ref, edge_ref, closing_ref, small_sem, edge_sem, closing_sem):
    small = [
        pltpu.make_async_copy(src, dst, small_sem.at[i])
        for i, (src, dst) in enumerate(((corner_hbm, corner_ref), (left_hbm, left_ref), (owner_hbm, owner_ref), (out_hbm, out_ref)))
    ]
    for copy in small:
        copy.start()
    big = []
    for t in range(TILES):
        rows = pl.ds(t * 2 * B, 2 * B)
        big.append((
            pltpu.make_async_copy(edge_hbm.at[rows], edge_ref.at[rows], edge_sem.at[t]),
            pltpu.make_async_copy(closing_hbm.at[rows], closing_ref.at[rows], closing_sem.at[t]),
        ))
    for t in range(AHEAD):
        big[t][0].start()
        big[t][1].start()

    low = low_lanes((B, 2 * B))
    small[0].wait()
    for r in range(2):
        for t in range(B // 2):
            rows_ref[r, pl.ds(t, 1), :] = corner_ref[pl.ds(r, 1), pl.ds(t * 2 * B, 2 * B)].astype(F32)
    low_half = low_lanes((B // 2, 2 * B))
    for r in range(2):
        packed = rows_ref[r]
        turned = pltpu.roll(packed, B, 1)
        both_ref[r, pl.ds(0, B // 2, stride=2), :] = jnp.where(low_half, packed, turned)
        both_ref[r, pl.ds(1, B // 2, stride=2), :] = jnp.where(low_half, turned, packed)
    small[1].wait()
    lefts = []
    for t in range(TILES):
        top = jnp.where(low, both_ref[left_ref[0, 2 * t]], 0.0)
        bottom = jnp.where(low, 0.0, both_ref[left_ref[0, 2 * t + 1]])
        lefts.append(jnp.concatenate([top, bottom], axis=0).astype(BF16))

    small[2].wait()
    for s in range(SECTORS - 1, -1, -1):
        first_ref[owner_ref[s]] = s
    small[3].wait()
    slots = []
    for k in range(PAIRS):
        sector = out_ref[0, k]
        own = owner_ref[sector]
        slots.append((2 * own + jnp.where(first_ref[own] == sector, 0, 1)).astype(F32))
    low_row = low_lanes((1, 2 * B))
    for t in range(TILES):
        a, b = slots[2 * t], slots[2 * t + 1]
        msg_ref[pl.ds(MSG + 2 * t, 1), :] = jnp.where(low_row, a, b)
        msg_ref[pl.ds(MSG + 2 * t + 1, 1), :] = jnp.where(low_row, b, a)

    for t in range(TILES):
        rows = pl.ds(t * 2 * B, 2 * B)
        big[t][0].wait()
        big[t][1].wait()
        if t + AHEAD < TILES:
            big[t + AHEAD][0].start()
            big[t + AHEAD][1].start()
        enlarged = jnp.dot(lefts[t], edge_ref[rows], preferred_element_type=F32).astype(BF16)
        total = lax.dot_general(enlarged, closing_ref[rows], (((1,), (1,)), ((), ())), preferred_element_type=F32)
        msg_ref[pl.ds(t * B, B), :] = jnp.where(low, total[:B], total[B:])


HOPS = ((4, -3), (3, -2), (1, 2), (0, -1))


def place_kernel(count, before, *all_refs):
    refs, all_refs = all_refs[:count], all_refs[count:]
    outs = len(HOPS) + 1
    before_refs, all_refs = all_refs[: outs * before], all_refs[outs * before :]
    out_refs, turned_ref = all_refs[:-1], all_refs[-1]
    for i, ref in enumerate(refs):
        for t in range(TILES):
            turned_ref[i, t] = pltpu.roll(ref[pl.ds(t * B, B), :], B, 1)
    core, z = lax.axis_index("core"), lax.axis_index("z")
    first = 4 * ZS * lax.axis_index("xl") + jnp.where(low_lanes((1, 2 * B)), 0, 1)

    def placed(step, to, total):
        slot = (first + 4 * ((z + step) & (ZS - 1)) + 2 * to).astype(F32)
        for i, ref in enumerate(refs):
            for t in range(TILES):
                straight = ref[pl.ds(MSG + 2 * t, 1), :] == slot
                crossed = ref[pl.ds(MSG + 2 * t + 1, 1), :] == slot
                total = total + jnp.where(straight, ref[pl.ds(t * B, B), :], 0.0)
                total = total + jnp.where(crossed, turned_ref[i, t], 0.0)
        return total

    zero = jnp.zeros((B, 2 * B), F32)
    for n, (even, odd) in enumerate(HOPS):
        step = jnp.where(core == 0, even, odd)
        out_refs[n][0] = placed(step, core, before_refs[n][0] if before else zero)
        out_refs[n][1] = placed(step, 1 - core, before_refs[n][1] if before else zero)
    out_refs[-1][...] = placed(0, core, before_refs[-1][...] if before else zero)


def gather_kernel(*refs):
    own_ref, out_ref = refs[-2:]
    out_ref[0] = refs[0][0] + refs[1][0] + refs[2][0] + refs[3][0] + own_ref[...]
    out_ref[1] = refs[0][1] + refs[1][1] + refs[2][1] + refs[3][1]


def project_kernel(mine_ref, beside_ref, projector_ref, other_ref, out_ref):
    low = low_lanes((B, 2 * B))

    def diagonal(packed):
        return jnp.concatenate([jnp.where(low, packed, 0.0), jnp.where(low, 0.0, packed)], axis=0)

    def project(joined, ref):
        proj = diagonal(jnp.concatenate([ref[0], ref[1]], axis=1))
        inner = jnp.dot(diagonal(joined), proj, precision=lax.Precision.HIGHEST, preferred_element_type=F32)
        full = lax.dot_general(proj, inner, (((0,), (0,)), ((), ())), precision=lax.Precision.HIGHEST, preferred_element_type=F32)
        return jnp.where(low, full[:B], full[B:])

    packed = project(mine_ref[0] + beside_ref[1], projector_ref)
    other = project(mine_ref[1] + beside_ref[0], other_ref)
    out_ref[pl.ds(0, B), :] = packed
    size = jnp.maximum(jnp.abs(packed), jnp.abs(other))
    top = size[:8]
    for i in range(1, 8):
        top = jnp.maximum(top, size[8 * i : 8 * i + 8])
    out_ref[pl.ds(B, 2 * ZS), :] = jnp.broadcast_to(jnp.max(top, axis=0, keepdims=True), (2 * ZS, 2 * B))


def finish_kernel(moved_ref, tops_ref, out_ref, rows_ref):
    scale = jnp.max(tops_ref[...]) + 1e-06
    low = low_lanes((B // 2, 2 * B))
    even = moved_ref[pl.ds(0, B // 2, stride=2), :] / scale
    odd = moved_ref[pl.ds(1, B // 2, stride=2), :] / scale
    rows_ref[0] = jnp.where(low, even, pltpu.roll(odd, B, 1))
    rows_ref[1] = jnp.where(low, pltpu.roll(even, B, 1), odd)
    for r in range(2):
        for t in range(B // 2):
            out_ref[pl.ds(r, 1), pl.ds(t * 2 * B, 2 * B)] = rows_ref[r, pl.ds(t, 1), :]


VMEM = pl.BlockSpec(memory_space=pltpu.VMEM)
ANY = pl.BlockSpec(memory_space=pl.ANY)
SMALL = pltpu.CompilerParams(vmem_limit_bytes=8 << 20)


def place(messages, before=()):
    tile, both = pltpu.VMEM((B, 2 * B), F32), pltpu.VMEM((2, B, 2 * B), F32)
    outs = len(HOPS) + 1
    return pl.pallas_call(
        functools.partial(place_kernel, len(messages), bool(before)),
        out_shape=[both] * len(HOPS) + [tile],
        in_specs=[VMEM] * (len(messages) + len(before)),
        out_specs=[VMEM] * outs,
        scratch_shapes=[pltpu.VMEM((len(messages), TILES, B, 2 * B), F32)],
        compiler_params=SMALL,
        name="place",
    )(*messages, *before)


def in_hbm(x):
    return pltpu.with_memory_space_constraint(x, pltpu.HBM)


def local(corner, edge, closing, projector, left_slot, out_sector, owner):
    message = pl.pallas_call(
        products_kernel,
        out_shape=pltpu.VMEM((MSG + PAIRS, 2 * B), F32),
        in_specs=[ANY] * 6,
        out_specs=VMEM,
        scratch_shapes=[
            pltpu.SMEM((1, PAIRS), jnp.int32),
            pltpu.SMEM((1, PAIRS), jnp.int32),
            pltpu.SMEM((SECTORS,), jnp.int32),
            pltpu.SMEM((SECTORS // 2,), jnp.int32),
            pltpu.VMEM((2, B * B), BF16),
            pltpu.VMEM((2, B // 2, 2 * B), F32),
            pltpu.VMEM((2, B, 2 * B), F32),
            pltpu.VMEM((PAIRS * B, WIDE), BF16),
            pltpu.VMEM((PAIRS * B, WIDE), BF16),
            pltpu.SemaphoreType.DMA((4,)),
            pltpu.SemaphoreType.DMA((TILES,)),
            pltpu.SemaphoreType.DMA((TILES,)),
        ],
        compiler_params=pltpu.CompilerParams(vmem_limit_bytes=24 << 20),
        name="products",
    )(*map(in_hbm, (left_slot, out_sector, owner, corner[0], edge.reshape(PAIRS * B, WIDE), closing.reshape(PAIRS * B, WIDE))))
    over = lax.ppermute(message, "xl", SWAP)
    beside = lax.ppermute(message, "core", SWAP)
    projector = projector.reshape(2, B, B)
    other = lax.ppermute(projector, "core", SWAP)
    over, projector, other = lax.optimization_barrier((over, projector, other))
    across = lax.ppermute(over, "core", SWAP)
    parts = place((message, beside))
    parts = place((over,), parts)
    *sent, own = place((across,), parts)
    both = pltpu.VMEM((2, B, 2 * B), F32)

    def along(x, steps):
        moves = [(2 * z + q, 2 * ((z + steps[q]) % ZS) + q) for z in range(ZS) for q in range(2) if steps[q]]
        return lax.ppermute(x, ("z", "core"), moves)

    came = [along(x, steps) for x, steps in zip(sent, HOPS)]
    mine = pl.pallas_call(gather_kernel, out_shape=both, in_specs=[VMEM] * (len(HOPS) + 1), out_specs=VMEM, compiler_params=SMALL, name="gather")(*came, own)
    beside = lax.ppermute(mine, "core", SWAP)
    payload = pl.pallas_call(
        project_kernel,
        out_shape=pltpu.VMEM((B + 2 * ZS, 2 * B), F32),
        in_specs=[VMEM] * 4,
        out_specs=VMEM,
        compiler_params=SMALL,
        name="project",
    )(mine, beside, projector, other)
    moved = lax.ppermute(payload, "col", [(i, (i + 1) % 8) for i in range(8)])
    tops = lax.all_to_all(moved[B:], ("xl", "z"), 0, 0, tiled=True)
    return pl.pallas_call(
        finish_kernel,
        out_shape=jax.ShapeDtypeStruct((2, B * B), F32),
        in_specs=[VMEM, VMEM],
        out_specs=VMEM,
        scratch_shapes=[pltpu.VMEM((2, B // 2, 2 * B), F32)],
        compiler_params=SMALL,
        name="finish",
    )(moved, tops)[None]


def solution(mesh):
    fine = Mesh(mesh.devices.reshape(8, 2, ZS, 2), ("col", "xl", "z", "core"))
    sec = ("xl", "z", "core")
    in_specs = (
        P("col", sec, None),
        P("col", sec, None, None),
        P("col", sec, None, None),
        P("col", sec, None),
        P("col", sec),
        P("col", sec),
        P(),
    )
    return jax.shard_map(local, mesh=fine, in_specs=in_specs, out_specs=P("col", sec, None), check_vma=False)
```

```python
import functools

import jax
import jax.numpy as jnp
from jax import lax
from jax.experimental import pallas as pl
from jax.experimental.pallas import tpu as pltpu
from jax.sharding import Mesh, PartitionSpec as P

B = 64
WIDE = 4096
PAIRS = 8
TILES = PAIRS // 2
MSG = TILES * B
SECTORS = 64
ZS = 8
AHEAD = 3
SWAP = [(0, 1), (1, 0)]
F32 = jnp.float32
BF16 = jnp.bfloat16


def low_lanes(shape):
    return lax.broadcasted_iota(jnp.int32, shape, len(shape) - 1) < B


def products_kernel(left_hbm, out_hbm, owner_hbm, corner_hbm, edge_hbm, closing_hbm, msg_ref, left_ref, out_ref, owner_ref, first_ref, corner_ref, rows_ref, both_ref, edge_ref, closing_ref, small_sem, edge_sem, closing_sem):
    small = [
        pltpu.make_async_copy(src, dst, small_sem.at[i])
        for i, (src, dst) in enumerate(((corner_hbm, corner_ref), (left_hbm, left_ref), (owner_hbm, owner_ref), (out_hbm, out_ref)))
    ]
    for copy in small:
        copy.start()
    big = []
    for t in range(TILES):
        rows = pl.ds(t * 2 * B, 2 * B)
        big.append((
            pltpu.make_async_copy(edge_hbm.at[rows], edge_ref.at[rows], edge_sem.at[t]),
            pltpu.make_async_copy(closing_hbm.at[rows], closing_ref.at[rows], closing_sem.at[t]),
        ))
    for t in range(AHEAD):
        big[t][0].start()
        big[t][1].start()

    low = low_lanes((B, 2 * B))
    small[0].wait()
    for r in range(2):
        for t in range(B // 2):
            rows_ref[r, pl.ds(t, 1), :] = corner_ref[pl.ds(r, 1), pl.ds(t * 2 * B, 2 * B)].astype(F32)
    low_half = low_lanes((B // 2, 2 * B))
    for r in range(2):
        packed = rows_ref[r]
        turned = pltpu.roll(packed, B, 1)
        both_ref[r, pl.ds(0, B // 2, stride=2), :] = jnp.where(low_half, packed, turned)
        both_ref[r, pl.ds(1, B // 2, stride=2), :] = jnp.where(low_half, turned, packed)
    small[1].wait()
    lefts = []
    for t in range(TILES):
        top = jnp.where(low, both_ref[left_ref[0, 2 * t]], 0.0)
        bottom = jnp.where(low, 0.0, both_ref[left_ref[0, 2 * t + 1]])
        lefts.append(jnp.concatenate([top, bottom], axis=0).astype(BF16))

    small[2].wait()
    for s in range(SECTORS - 1, -1, -1):
        first_ref[owner_ref[s]] = s
    small[3].wait()
    slots = []
    for k in range(PAIRS):
        sector = out_ref[0, k]
        own = owner_ref[sector]
        slots.append((2 * own + jnp.where(first_ref[own] == sector, 0, 1)).astype(F32))
    low_row = low_lanes((1, 2 * B))
    for t in range(TILES):
        a, b = slots[2 * t], slots[2 * t + 1]
        msg_ref[pl.ds(MSG + 2 * t, 1), :] = jnp.where(low_row, a, b)
        msg_ref[pl.ds(MSG + 2 * t + 1, 1), :] = jnp.where(low_row, b, a)

    for t in range(TILES):
        rows = pl.ds(t * 2 * B, 2 * B)
        big[t][0].wait()
        big[t][1].wait()
        if t + AHEAD < TILES:
            big[t + AHEAD][0].start()
            big[t + AHEAD][1].start()
        enlarged = jnp.dot(lefts[t], edge_ref[rows], preferred_element_type=F32).astype(BF16)
        total = lax.dot_general(enlarged, closing_ref[rows], (((1,), (1,)), ((), ())), preferred_element_type=F32)
        msg_ref[pl.ds(t * B, B), :] = jnp.where(low, total[:B], total[B:])


LEAD = [8 * x + z for z in range(ZS - 1, -1, -1) for x in range(2)]
HOPS = ((4, -3), (3, -2), (-1, 2), (0, 1))


def place_kernel(count, before, *all_refs):
    refs, all_refs = all_refs[:count], all_refs[count:]
    outs = len(HOPS) + 1
    before_refs, all_refs = all_refs[: outs * before], all_refs[outs * before :]
    out_refs, turned_ref = all_refs[:-1], all_refs[-1]
    for i, ref in enumerate(refs):
        for t in range(TILES):
            turned_ref[i, t] = pltpu.roll(ref[pl.ds(t * B, B), :], B, 1)
    core, z = lax.axis_index("core"), lax.axis_index("z")
    first = 4 * ZS * lax.axis_index("xl") + jnp.where(low_lanes((1, 2 * B)), 0, 1)

    def placed(step, to, total):
        slot = (first + 4 * ((z + step) & (ZS - 1)) + 2 * to).astype(F32)
        for i, ref in enumerate(refs):
            for t in range(TILES):
                straight = ref[pl.ds(MSG + 2 * t, 1), :] == slot
                crossed = ref[pl.ds(MSG + 2 * t + 1, 1), :] == slot
                total = total + jnp.where(straight, ref[pl.ds(t * B, B), :], 0.0)
                total = total + jnp.where(crossed, turned_ref[i, t], 0.0)
        return total

    zero = jnp.zeros((B, 2 * B), F32)
    for n, (even, odd) in enumerate(HOPS):
        step = jnp.where(core == 0, even, odd)
        out_refs[n][0] = placed(step, core, before_refs[n][0] if before else zero)
        out_refs[n][1] = placed(step, 1 - core, before_refs[n][1] if before else zero)
    out_refs[-1][...] = placed(0, core, before_refs[-1][...] if before else zero)


def gather_kernel(*refs):
    own_ref, out_ref = refs[-2:]
    out_ref[0] = refs[0][0] + refs[1][0] + refs[2][0] + refs[3][0] + own_ref[...]
    out_ref[1] = refs[0][1] + refs[1][1] + refs[2][1] + refs[3][1]


def project_kernel(mine_ref, beside_ref, projector_ref, other_ref, out_ref):
    low = low_lanes((B, 2 * B))

    def diagonal(packed):
        return jnp.concatenate([jnp.where(low, packed, 0.0), jnp.where(low, 0.0, packed)], axis=0)

    def project(joined, ref):
        proj = diagonal(jnp.concatenate([ref[0], ref[1]], axis=1))
        inner = jnp.dot(diagonal(joined), proj, precision=lax.Precision.HIGHEST, preferred_element_type=F32)
        full = lax.dot_general(proj, inner, (((0,), (0,)), ((), ())), precision=lax.Precision.HIGHEST, preferred_element_type=F32)
        return jnp.where(low, full[:B], full[B:])

    packed = project(mine_ref[0] + beside_ref[1], projector_ref)
    other = project(mine_ref[1] + beside_ref[0], other_ref)
    out_ref[pl.ds(0, B), :] = packed
    size = jnp.maximum(jnp.abs(packed), jnp.abs(other))
    top = size[:8]
    for i in range(1, 8):
        top = jnp.maximum(top, size[8 * i : 8 * i + 8])
    out_ref[pl.ds(B, 2 * ZS), :] = jnp.broadcast_to(jnp.max(top, axis=0, keepdims=True), (2 * ZS, 2 * B))


def finish_kernel(moved_ref, tops_ref, out_ref, rows_ref):
    scale = jnp.max(tops_ref[...]) + 1e-06
    low = low_lanes((B // 2, 2 * B))
    even = moved_ref[pl.ds(0, B // 2, stride=2), :] / scale
    odd = moved_ref[pl.ds(1, B // 2, stride=2), :] / scale
    rows_ref[0] = jnp.where(low, even, pltpu.roll(odd, B, 1))
    rows_ref[1] = jnp.where(low, pltpu.roll(even, B, 1), odd)
    for r in range(2):
        for t in range(B // 2):
            out_ref[pl.ds(r, 1), pl.ds(t * 2 * B, 2 * B)] = rows_ref[r, pl.ds(t, 1), :]


VMEM = pl.BlockSpec(memory_space=pltpu.VMEM)
ANY = pl.BlockSpec(memory_space=pl.ANY)
SMALL = pltpu.CompilerParams(vmem_limit_bytes=8 << 20)


def place(messages, before=()):
    tile, both = pltpu.VMEM((B, 2 * B), F32), pltpu.VMEM((2, B, 2 * B), F32)
    outs = len(HOPS) + 1
    return pl.pallas_call(
        functools.partial(place_kernel, len(messages), bool(before)),
        out_shape=[both] * len(HOPS) + [tile],
        in_specs=[VMEM] * (len(messages) + len(before)),
        out_specs=[VMEM] * outs,
        scratch_shapes=[pltpu.VMEM((len(messages), TILES, B, 2 * B), F32)],
        compiler_params=SMALL,
        name="place",
    )(*messages, *before)


def in_hbm(x):
    return pltpu.with_memory_space_constraint(x, pltpu.HBM)


def local(corner, edge, closing, projector, left_slot, out_sector, owner):
    message = pl.pallas_call(
        products_kernel,
        out_shape=pltpu.VMEM((MSG + PAIRS, 2 * B), F32),
        in_specs=[ANY] * 6,
        out_specs=VMEM,
        scratch_shapes=[
            pltpu.SMEM((1, PAIRS), jnp.int32),
            pltpu.SMEM((1, PAIRS), jnp.int32),
            pltpu.SMEM((SECTORS,), jnp.int32),
            pltpu.SMEM((SECTORS // 2,), jnp.int32),
            pltpu.VMEM((2, B * B), BF16),
            pltpu.VMEM((2, B // 2, 2 * B), F32),
            pltpu.VMEM((2, B, 2 * B), F32),
            pltpu.VMEM((PAIRS * B, WIDE), BF16),
            pltpu.VMEM((PAIRS * B, WIDE), BF16),
            pltpu.SemaphoreType.DMA((4,)),
            pltpu.SemaphoreType.DMA((TILES,)),
            pltpu.SemaphoreType.DMA((TILES,)),
        ],
        compiler_params=pltpu.CompilerParams(vmem_limit_bytes=24 << 20),
        name="products",
    )(*map(in_hbm, (left_slot, out_sector, owner, corner[0], edge.reshape(PAIRS * B, WIDE), closing.reshape(PAIRS * B, WIDE))))
    over = lax.ppermute(message, "xl", SWAP)
    beside = lax.ppermute(message, "core", SWAP)
    projector = projector.reshape(2, B, B)
    other = lax.ppermute(projector, "core", SWAP)
    over, projector, other = lax.optimization_barrier((over, projector, other))
    across = lax.ppermute(over, "core", SWAP)
    parts = place((message, beside))
    parts = place((over,), parts)
    *sent, own = place((across,), parts)
    both = pltpu.VMEM((2, B, 2 * B), F32)

    def along(x, steps):
        moves = [(2 * z + q, 2 * ((z + steps[q]) % ZS) + q) for z in range(ZS) for q in range(2) if steps[q]]
        return lax.ppermute(x, ("z", "core"), moves)

    came = [along(x, steps) for x, steps in zip(sent, HOPS)]
    mine = pl.pallas_call(gather_kernel, out_shape=both, in_specs=[VMEM] * (len(HOPS) + 1), out_specs=VMEM, compiler_params=SMALL, name="gather")(*came, own)
    beside = lax.ppermute(mine, "core", SWAP)
    payload = pl.pallas_call(
        project_kernel,
        out_shape=pltpu.VMEM((B + 2 * ZS, 2 * B), F32),
        in_specs=[VMEM] * 4,
        out_specs=VMEM,
        compiler_params=SMALL,
        name="project",
    )(mine, beside, projector, other)
    moved = lax.ppermute(payload, "col", [(i, (i + 1) % 8) for i in range(8)])
    tops = lax.all_to_all(moved[B:], ("xl", "z"), 0, 0, tiled=True, axis_index_groups=[LEAD])
    return pl.pallas_call(
        finish_kernel,
        out_shape=jax.ShapeDtypeStruct((2, B * B), F32),
        in_specs=[VMEM, VMEM],
        out_specs=VMEM,
        scratch_shapes=[pltpu.VMEM((2, B // 2, 2 * B), F32)],
        compiler_params=SMALL,
        name="finish",
    )(moved, tops)[None]


def solution(mesh):
    fine = Mesh(mesh.devices.reshape(8, 2, ZS, 2), ("col", "xl", "z", "core"))
    sec = ("xl", "z", "core")
    in_specs = (
        P("col", sec, None),
        P("col", sec, None, None),
        P("col", sec, None, None),
        P("col", sec, None),
        P("col", sec),
        P("col", sec),
        P(),
    )
    return jax.shard_map(local, mesh=fine, in_specs=in_specs, out_specs=P("col", sec, None), check_vma=False)
```

```python
import functools

import jax
import jax.numpy as jnp
from jax import lax
from jax.experimental import pallas as pl
from jax.experimental.pallas import tpu as pltpu
from jax.sharding import Mesh, PartitionSpec as P

B = 64
WIDE = 4096
PAIRS = 8
TILES = PAIRS // 2
MSG = TILES * B
SECTORS = 64
ZS = 8
AHEAD = 3
SWAP = [(0, 1), (1, 0)]
F32 = jnp.float32
BF16 = jnp.bfloat16


def low_lanes(shape):
    return lax.broadcasted_iota(jnp.int32, shape, len(shape) - 1) < B


def products_kernel(left_hbm, out_hbm, owner_hbm, corner_hbm, edge_hbm, closing_hbm, msg_ref, left_ref, out_ref, owner_ref, first_ref, corner_ref, rows_ref, both_ref, edge_ref, closing_ref, small_sem, edge_sem, closing_sem):
    small = [
        pltpu.make_async_copy(src, dst, small_sem.at[i])
        for i, (src, dst) in enumerate(((corner_hbm, corner_ref), (left_hbm, left_ref), (owner_hbm, owner_ref), (out_hbm, out_ref)))
    ]
    for copy in small:
        copy.start()
    big = []
    for t in range(TILES):
        rows = pl.ds(t * 2 * B, 2 * B)
        big.append((
            pltpu.make_async_copy(edge_hbm.at[rows], edge_ref.at[rows], edge_sem.at[t]),
            pltpu.make_async_copy(closing_hbm.at[rows], closing_ref.at[rows], closing_sem.at[t]),
        ))
    for t in range(AHEAD):
        big[t][0].start()
        big[t][1].start()

    low = low_lanes((B, 2 * B))
    small[0].wait()
    for r in range(2):
        for t in range(B // 2):
            rows_ref[r, pl.ds(t, 1), :] = corner_ref[pl.ds(r, 1), pl.ds(t * 2 * B, 2 * B)].astype(F32)
    low_half = low_lanes((B // 2, 2 * B))
    for r in range(2):
        packed = rows_ref[r]
        turned = pltpu.roll(packed, B, 1)
        both_ref[r, pl.ds(0, B // 2, stride=2), :] = jnp.where(low_half, packed, turned)
        both_ref[r, pl.ds(1, B // 2, stride=2), :] = jnp.where(low_half, turned, packed)
    small[1].wait()
    lefts = []
    for t in range(TILES):
        top = jnp.where(low, both_ref[left_ref[0, 2 * t]], 0.0)
        bottom = jnp.where(low, 0.0, both_ref[left_ref[0, 2 * t + 1]])
        lefts.append(jnp.concatenate([top, bottom], axis=0).astype(BF16))

    small[2].wait()
    for s in range(SECTORS - 1, -1, -1):
        first_ref[owner_ref[s]] = s
    small[3].wait()
    slots = []
    for k in range(PAIRS):
        sector = out_ref[0, k]
        own = owner_ref[sector]
        slots.append((2 * own + jnp.where(first_ref[own] == sector, 0, 1)).astype(F32))
    low_row = low_lanes((1, 2 * B))
    for t in range(TILES):
        a, b = slots[2 * t], slots[2 * t + 1]
        msg_ref[pl.ds(MSG + 2 * t, 1), :] = jnp.where(low_row, a, b)
        msg_ref[pl.ds(MSG + 2 * t + 1, 1), :] = jnp.where(low_row, b, a)

    for t in range(TILES):
        rows = pl.ds(t * 2 * B, 2 * B)
        big[t][0].wait()
        big[t][1].wait()
        if t + AHEAD < TILES:
            big[t + AHEAD][0].start()
            big[t + AHEAD][1].start()
        enlarged = jnp.dot(lefts[t], edge_ref[rows], preferred_element_type=F32).astype(BF16)
        total = lax.dot_general(enlarged, closing_ref[rows], (((1,), (1,)), ((), ())), preferred_element_type=F32)
        msg_ref[pl.ds(t * B, B), :] = jnp.where(low, total[:B], total[B:])


LEAD = [8 * x + z for z in (5, 4, 3, 2, 1, 0, 7, 6) for x in range(2)]
HOPS = ((4, -3), (-2, 3), (-1, 2), (0, 1))


def place_kernel(count, before, *all_refs):
    refs, all_refs = all_refs[:count], all_refs[count:]
    outs = len(HOPS) + 1
    before_refs, all_refs = all_refs[: outs * before], all_refs[outs * before :]
    out_refs, turned_ref = all_refs[:-1], all_refs[-1]
    for i, ref in enumerate(refs):
        for t in range(TILES):
            turned_ref[i, t] = pltpu.roll(ref[pl.ds(t * B, B), :], B, 1)
    core, z = lax.axis_index("core"), lax.axis_index("z")
    first = 4 * ZS * lax.axis_index("xl") + jnp.where(low_lanes((1, 2 * B)), 0, 1)

    def placed(step, to, total):
        slot = (first + 4 * ((z + step) & (ZS - 1)) + 2 * to).astype(F32)
        for i, ref in enumerate(refs):
            for t in range(TILES):
                straight = ref[pl.ds(MSG + 2 * t, 1), :] == slot
                crossed = ref[pl.ds(MSG + 2 * t + 1, 1), :] == slot
                total = total + jnp.where(straight, ref[pl.ds(t * B, B), :], 0.0)
                total = total + jnp.where(crossed, turned_ref[i, t], 0.0)
        return total

    zero = jnp.zeros((B, 2 * B), F32)
    for n, (even, odd) in enumerate(HOPS):
        step = jnp.where(core == 0, even, odd)
        out_refs[n][0] = placed(step, core, before_refs[n][0] if before else zero)
        out_refs[n][1] = placed(step, 1 - core, before_refs[n][1] if before else zero)
    out_refs[-1][...] = placed(0, core, before_refs[-1][...] if before else zero)


def gather_kernel(*refs):
    own_ref, out_ref = refs[-2:]
    out_ref[0] = refs[0][0] + refs[1][0] + refs[2][0] + refs[3][0] + own_ref[...]
    out_ref[1] = refs[0][1] + refs[1][1] + refs[2][1] + refs[3][1]


def project_kernel(mine_ref, beside_ref, projector_ref, other_ref, out_ref):
    low = low_lanes((B, 2 * B))

    def diagonal(packed):
        return jnp.concatenate([jnp.where(low, packed, 0.0), jnp.where(low, 0.0, packed)], axis=0)

    def project(joined, ref):
        proj = diagonal(jnp.concatenate([ref[0], ref[1]], axis=1))
        inner = jnp.dot(diagonal(joined), proj, precision=lax.Precision.HIGHEST, preferred_element_type=F32)
        full = lax.dot_general(proj, inner, (((0,), (0,)), ((), ())), precision=lax.Precision.HIGHEST, preferred_element_type=F32)
        return jnp.where(low, full[:B], full[B:])

    packed = project(mine_ref[0] + beside_ref[1], projector_ref)
    other = project(mine_ref[1] + beside_ref[0], other_ref)
    out_ref[pl.ds(0, B), :] = packed
    size = jnp.maximum(jnp.abs(packed), jnp.abs(other))
    top = size[:8]
    for i in range(1, 8):
        top = jnp.maximum(top, size[8 * i : 8 * i + 8])
    out_ref[pl.ds(B, 2 * ZS), :] = jnp.broadcast_to(jnp.max(top, axis=0, keepdims=True), (2 * ZS, 2 * B))


def finish_kernel(moved_ref, tops_ref, out_ref, rows_ref):
    scale = jnp.max(tops_ref[...]) + 1e-06
    low = low_lanes((B // 2, 2 * B))
    even = moved_ref[pl.ds(0, B // 2, stride=2), :] / scale
    odd = moved_ref[pl.ds(1, B // 2, stride=2), :] / scale
    rows_ref[0] = jnp.where(low, even, pltpu.roll(odd, B, 1))
    rows_ref[1] = jnp.where(low, pltpu.roll(even, B, 1), odd)
    for r in range(2):
        for t in range(B // 2):
            out_ref[pl.ds(r, 1), pl.ds(t * 2 * B, 2 * B)] = rows_ref[r, pl.ds(t, 1), :]


VMEM = pl.BlockSpec(memory_space=pltpu.VMEM)
ANY = pl.BlockSpec(memory_space=pl.ANY)
SMALL = pltpu.CompilerParams(vmem_limit_bytes=8 << 20)


def place(messages, before=()):
    tile, both = pltpu.VMEM((B, 2 * B), F32), pltpu.VMEM((2, B, 2 * B), F32)
    outs = len(HOPS) + 1
    return pl.pallas_call(
        functools.partial(place_kernel, len(messages), bool(before)),
        out_shape=[both] * len(HOPS) + [tile],
        in_specs=[VMEM] * (len(messages) + len(before)),
        out_specs=[VMEM] * outs,
        scratch_shapes=[pltpu.VMEM((len(messages), TILES, B, 2 * B), F32)],
        compiler_params=SMALL,
        name="place",
    )(*messages, *before)


def in_hbm(x):
    return pltpu.with_memory_space_constraint(x, pltpu.HBM)


def local(corner, edge, closing, projector, left_slot, out_sector, owner):
    message = pl.pallas_call(
        products_kernel,
        out_shape=pltpu.VMEM((MSG + PAIRS, 2 * B), F32),
        in_specs=[ANY] * 6,
        out_specs=VMEM,
        scratch_shapes=[
            pltpu.SMEM((1, PAIRS), jnp.int32),
            pltpu.SMEM((1, PAIRS), jnp.int32),
            pltpu.SMEM((SECTORS,), jnp.int32),
            pltpu.SMEM((SECTORS // 2,), jnp.int32),
            pltpu.VMEM((2, B * B), BF16),
            pltpu.VMEM((2, B // 2, 2 * B), F32),
            pltpu.VMEM((2, B, 2 * B), F32),
            pltpu.VMEM((PAIRS * B, WIDE), BF16),
            pltpu.VMEM((PAIRS * B, WIDE), BF16),
            pltpu.SemaphoreType.DMA((4,)),
            pltpu.SemaphoreType.DMA((TILES,)),
            pltpu.SemaphoreType.DMA((TILES,)),
        ],
        compiler_params=pltpu.CompilerParams(vmem_limit_bytes=24 << 20),
        name="products",
    )(*map(in_hbm, (left_slot, out_sector, owner, corner[0], edge.reshape(PAIRS * B, WIDE), closing.reshape(PAIRS * B, WIDE))))
    over = lax.ppermute(message, "xl", SWAP)
    beside = lax.ppermute(message, "core", SWAP)
    projector = projector.reshape(2, B, B)
    other = lax.ppermute(projector, "core", SWAP)
    over, projector, other = lax.optimization_barrier((over, projector, other))
    across = lax.ppermute(over, "core", SWAP)
    parts = place((message, beside))
    parts = place((over,), parts)
    *sent, own = place((across,), parts)
    both = pltpu.VMEM((2, B, 2 * B), F32)

    def along(x, steps):
        moves = [(2 * z + q, 2 * ((z + steps[q]) % ZS) + q) for z in range(ZS) for q in range(2) if steps[q]]
        return lax.ppermute(x, ("z", "core"), moves)

    came = [along(x, steps) for x, steps in zip(sent, HOPS)]
    mine = pl.pallas_call(gather_kernel, out_shape=both, in_specs=[VMEM] * (len(HOPS) + 1), out_specs=VMEM, compiler_params=SMALL, name="gather")(*came, own)
    beside = lax.ppermute(mine, "core", SWAP)
    payload = pl.pallas_call(
        project_kernel,
        out_shape=pltpu.VMEM((B + 2 * ZS, 2 * B), F32),
        in_specs=[VMEM] * 4,
        out_specs=VMEM,
        compiler_params=SMALL,
        name="project",
    )(mine, beside, projector, other)
    moved = lax.ppermute(payload, "col", [(i, (i + 1) % 8) for i in range(8)])
    tops = lax.all_to_all(moved[B:], ("xl", "z"), 0, 0, tiled=True, axis_index_groups=[LEAD])
    return pl.pallas_call(
        finish_kernel,
        out_shape=jax.ShapeDtypeStruct((2, B * B), F32),
        in_specs=[VMEM, VMEM],
        out_specs=VMEM,
        scratch_shapes=[pltpu.VMEM((2, B // 2, 2 * B), F32)],
        compiler_params=SMALL,
        name="finish",
    )(moved, tops)[None]


def solution(mesh):
    fine = Mesh(mesh.devices.reshape(8, 2, ZS, 2), ("col", "xl", "z", "core"))
    sec = ("xl", "z", "core")
    in_specs = (
        P("col", sec, None),
        P("col", sec, None, None),
        P("col", sec, None, None),
        P("col", sec, None),
        P("col", sec),
        P("col", sec),
        P(),
    )
    return jax.shard_map(local, mesh=fine, in_specs=in_specs, out_specs=P("col", sec, None), check_vma=False)
```

```python
import functools

import jax
import jax.numpy as jnp
from jax import lax
from jax.experimental import pallas as pl
from jax.experimental.pallas import tpu as pltpu
from jax.sharding import Mesh, PartitionSpec as P

B = 64
WIDE = 4096
PAIRS = 8
TILES = PAIRS // 2
MSG = TILES * B
SECTORS = 64
ZS = 8
AHEAD = 3
SWAP = [(0, 1), (1, 0)]
F32 = jnp.float32
BF16 = jnp.bfloat16


def low_lanes(shape):
    return lax.broadcasted_iota(jnp.int32, shape, len(shape) - 1) < B


def products_kernel(left_hbm, out_hbm, owner_hbm, corner_hbm, edge_hbm, closing_hbm, msg_ref, left_ref, out_ref, owner_ref, first_ref, corner_ref, rows_ref, both_ref, edge_ref, closing_ref, small_sem, edge_sem, closing_sem):
    small = [
        pltpu.make_async_copy(src, dst, small_sem.at[i])
        for i, (src, dst) in enumerate(((corner_hbm, corner_ref), (left_hbm, left_ref), (owner_hbm, owner_ref), (out_hbm, out_ref)))
    ]
    for copy in small:
        copy.start()
    big = []
    for t in range(TILES):
        rows = pl.ds(t * 2 * B, 2 * B)
        big.append((
            pltpu.make_async_copy(edge_hbm.at[rows], edge_ref.at[rows], edge_sem.at[t]),
            pltpu.make_async_copy(closing_hbm.at[rows], closing_ref.at[rows], closing_sem.at[t]),
        ))
    for t in range(AHEAD):
        big[t][0].start()
        big[t][1].start()

    low = low_lanes((B, 2 * B))
    small[0].wait()
    for r in range(2):
        for t in range(B // 2):
            rows_ref[r, pl.ds(t, 1), :] = corner_ref[pl.ds(r, 1), pl.ds(t * 2 * B, 2 * B)].astype(F32)
    low_half = low_lanes((B // 2, 2 * B))
    for r in range(2):
        packed = rows_ref[r]
        turned = pltpu.roll(packed, B, 1)
        both_ref[r, pl.ds(0, B // 2, stride=2), :] = jnp.where(low_half, packed, turned)
        both_ref[r, pl.ds(1, B // 2, stride=2), :] = jnp.where(low_half, turned, packed)
    small[1].wait()
    lefts = []
    for t in range(TILES):
        top = jnp.where(low, both_ref[left_ref[0, 2 * t]], 0.0)
        bottom = jnp.where(low, 0.0, both_ref[left_ref[0, 2 * t + 1]])
        lefts.append(jnp.concatenate([top, bottom], axis=0).astype(BF16))

    small[2].wait()
    for s in range(SECTORS - 1, -1, -1):
        first_ref[owner_ref[s]] = s
    small[3].wait()
    slots = []
    for k in range(PAIRS):
        sector = out_ref[0, k]
        own = owner_ref[sector]
        slots.append((2 * own + jnp.where(first_ref[own] == sector, 0, 1)).astype(F32))
    low_row = low_lanes((1, 2 * B))
    for t in range(TILES):
        a, b = slots[2 * t], slots[2 * t + 1]
        msg_ref[pl.ds(MSG + 2 * t, 1), :] = jnp.where(low_row, a, b)
        msg_ref[pl.ds(MSG + 2 * t + 1, 1), :] = jnp.where(low_row, b, a)

    for t in range(TILES):
        rows = pl.ds(t * 2 * B, 2 * B)
        big[t][0].wait()
        big[t][1].wait()
        if t + AHEAD < TILES:
            big[t + AHEAD][0].start()
            big[t + AHEAD][1].start()
        enlarged = jnp.dot(lefts[t], edge_ref[rows], preferred_element_type=F32).astype(BF16)
        total = lax.dot_general(enlarged, closing_ref[rows], (((1,), (1,)), ((), ())), preferred_element_type=F32)
        msg_ref[pl.ds(t * B, B), :] = jnp.where(low, total[:B], total[B:])


LEAD = [8 * x + z for z in (5, 4, 3, 2, 1, 0, 7, 6) for x in range(2)]
HOPS = ((4, -3), (-2, 3), (-1, 2), (0, 1))


def place_kernel(count, before, *all_refs):
    refs, all_refs = all_refs[:count], all_refs[count:]
    outs = len(HOPS) + 1
    before_refs, all_refs = all_refs[: outs * before], all_refs[outs * before :]
    out_refs, turned_ref = all_refs[:-1], all_refs[-1]
    for i, ref in enumerate(refs):
        for t in range(TILES):
            turned_ref[i, t] = pltpu.roll(ref[pl.ds(t * B, B), :], B, 1)
    core, z = lax.axis_index("core"), lax.axis_index("z")
    first = 4 * ZS * lax.axis_index("xl") + jnp.where(low_lanes((1, 2 * B)), 0, 1)

    def placed(step, to, total):
        slot = (first + 4 * ((z + step) & (ZS - 1)) + 2 * to).astype(F32)
        for i, ref in enumerate(refs):
            for t in range(TILES):
                straight = ref[pl.ds(MSG + 2 * t, 1), :] == slot
                crossed = ref[pl.ds(MSG + 2 * t + 1, 1), :] == slot
                total = total + jnp.where(straight, ref[pl.ds(t * B, B), :], 0.0)
                total = total + jnp.where(crossed, turned_ref[i, t], 0.0)
        return total

    zero = jnp.zeros((B, 2 * B), F32)
    for n, (even, odd) in enumerate(HOPS):
        step = jnp.where(core == 0, even, odd)
        out_refs[n][0] = placed(step, core, before_refs[n][0] if before else zero)
        out_refs[n][1] = placed(step, 1 - core, before_refs[n][1] if before else zero)
    out_refs[-1][...] = placed(0, core, before_refs[-1][...] if before else zero)


def gather_kernel(*refs):
    own_ref, out_ref = refs[-2:]
    out_ref[0] = refs[0][0] + refs[1][0] + refs[2][0] + refs[3][0] + own_ref[...]
    out_ref[1] = refs[0][1] + refs[1][1] + refs[2][1] + refs[3][1]


def diagonal(packed):
    low = low_lanes((B, 2 * B))
    return jnp.concatenate([jnp.where(low, packed, 0.0), jnp.where(low, 0.0, packed)], axis=0)


def prepare_kernel(mine_ref, other_ref, right_ref, left_ref):
    for q, ref in enumerate((mine_ref, other_ref)):
        proj = diagonal(jnp.concatenate([ref[0], ref[1]], axis=1))
        right_ref[q] = proj
        left_ref[q] = proj.T


def project_kernel(mine_ref, beside_ref, right_ref, left_ref, out_ref):
    low = low_lanes((B, 2 * B))

    def project(joined, q):
        inner = jnp.dot(diagonal(joined), right_ref[q], precision=lax.Precision.HIGHEST, preferred_element_type=F32)
        full = jnp.dot(left_ref[q], inner, precision=lax.Precision.HIGHEST, preferred_element_type=F32)
        return jnp.where(low, full[:B], full[B:])

    packed = project(mine_ref[0] + beside_ref[1], 0)
    other = project(mine_ref[1] + beside_ref[0], 1)
    out_ref[pl.ds(0, B), :] = packed
    size = jnp.maximum(jnp.abs(packed), jnp.abs(other))
    top = size[:8]
    for i in range(1, 8):
        top = jnp.maximum(top, size[8 * i : 8 * i + 8])
    out_ref[pl.ds(B, 2 * ZS), :] = jnp.broadcast_to(jnp.max(top, axis=0, keepdims=True), (2 * ZS, 2 * B))


def finish_kernel(moved_ref, tops_ref, out_ref, rows_ref):
    scale = jnp.max(tops_ref[...]) + 1e-06
    low = low_lanes((B // 2, 2 * B))
    even = moved_ref[pl.ds(0, B // 2, stride=2), :] / scale
    odd = moved_ref[pl.ds(1, B // 2, stride=2), :] / scale
    rows_ref[0] = jnp.where(low, even, pltpu.roll(odd, B, 1))
    rows_ref[1] = jnp.where(low, pltpu.roll(even, B, 1), odd)
    for r in range(2):
        for t in range(B // 2):
            out_ref[pl.ds(r, 1), pl.ds(t * 2 * B, 2 * B)] = rows_ref[r, pl.ds(t, 1), :]


VMEM = pl.BlockSpec(memory_space=pltpu.VMEM)
ANY = pl.BlockSpec(memory_space=pl.ANY)
SMALL = pltpu.CompilerParams(vmem_limit_bytes=8 << 20)


def place(messages, before=()):
    tile, both = pltpu.VMEM((B, 2 * B), F32), pltpu.VMEM((2, B, 2 * B), F32)
    outs = len(HOPS) + 1
    return pl.pallas_call(
        functools.partial(place_kernel, len(messages), bool(before)),
        out_shape=[both] * len(HOPS) + [tile],
        in_specs=[VMEM] * (len(messages) + len(before)),
        out_specs=[VMEM] * outs,
        scratch_shapes=[pltpu.VMEM((len(messages), TILES, B, 2 * B), F32)],
        compiler_params=SMALL,
        name="place",
    )(*messages, *before)


def in_hbm(x):
    return pltpu.with_memory_space_constraint(x, pltpu.HBM)


def local(corner, edge, closing, projector, left_slot, out_sector, owner):
    message = pl.pallas_call(
        products_kernel,
        out_shape=pltpu.VMEM((MSG + PAIRS, 2 * B), F32),
        in_specs=[ANY] * 6,
        out_specs=VMEM,
        scratch_shapes=[
            pltpu.SMEM((1, PAIRS), jnp.int32),
            pltpu.SMEM((1, PAIRS), jnp.int32),
            pltpu.SMEM((SECTORS,), jnp.int32),
            pltpu.SMEM((SECTORS // 2,), jnp.int32),
            pltpu.VMEM((2, B * B), BF16),
            pltpu.VMEM((2, B // 2, 2 * B), F32),
            pltpu.VMEM((2, B, 2 * B), F32),
            pltpu.VMEM((PAIRS * B, WIDE), BF16),
            pltpu.VMEM((PAIRS * B, WIDE), BF16),
            pltpu.SemaphoreType.DMA((4,)),
            pltpu.SemaphoreType.DMA((TILES,)),
            pltpu.SemaphoreType.DMA((TILES,)),
        ],
        compiler_params=pltpu.CompilerParams(vmem_limit_bytes=24 << 20),
        name="products",
    )(*map(in_hbm, (left_slot, out_sector, owner, corner[0], edge.reshape(PAIRS * B, WIDE), closing.reshape(PAIRS * B, WIDE))))
    over = lax.ppermute(message, "xl", SWAP)
    beside = lax.ppermute(message, "core", SWAP)
    projector = projector.reshape(2, B, B)
    other = lax.ppermute(projector, "core", SWAP)
    right, left = pl.pallas_call(
        prepare_kernel,
        out_shape=[pltpu.VMEM((2, 2 * B, 2 * B), F32)] * 2,
        in_specs=[VMEM] * 2,
        out_specs=[VMEM] * 2,
        compiler_params=SMALL,
        name="prepare",
    )(projector, other)
    over, right, left = lax.optimization_barrier((over, right, left))
    across = lax.ppermute(over, "core", SWAP)
    parts = place((message, beside))
    parts = place((over,), parts)
    *sent, own = place((across,), parts)
    both = pltpu.VMEM((2, B, 2 * B), F32)

    def along(x, steps):
        moves = [(2 * z + q, 2 * ((z + steps[q]) % ZS) + q) for z in range(ZS) for q in range(2) if steps[q]]
        return lax.ppermute(x, ("z", "core"), moves)

    came = [along(x, steps) for x, steps in zip(sent, HOPS)]
    mine = pl.pallas_call(gather_kernel, out_shape=both, in_specs=[VMEM] * (len(HOPS) + 1), out_specs=VMEM, compiler_params=SMALL, name="gather")(*came, own)
    beside = lax.ppermute(mine, "core", SWAP)
    payload = pl.pallas_call(
        project_kernel,
        out_shape=pltpu.VMEM((B + 2 * ZS, 2 * B), F32),
        in_specs=[VMEM] * 4,
        out_specs=VMEM,
        compiler_params=SMALL,
        name="project",
    )(mine, beside, right, left)
    moved = lax.ppermute(payload, "col", [(i, (i + 1) % 8) for i in range(8)])
    tops = lax.all_to_all(moved[B:], ("xl", "z"), 0, 0, tiled=True, axis_index_groups=[LEAD])
    return pl.pallas_call(
        finish_kernel,
        out_shape=jax.ShapeDtypeStruct((2, B * B), F32),
        in_specs=[VMEM, VMEM],
        out_specs=VMEM,
        scratch_shapes=[pltpu.VMEM((2, B // 2, 2 * B), F32)],
        compiler_params=SMALL,
        name="finish",
    )(moved, tops)[None]


def solution(mesh):
    fine = Mesh(mesh.devices.reshape(8, 2, ZS, 2), ("col", "xl", "z", "core"))
    sec = ("xl", "z", "core")
    in_specs = (
        P("col", sec, None),
        P("col", sec, None, None),
        P("col", sec, None, None),
        P("col", sec, None),
        P("col", sec),
        P("col", sec),
        P(),
    )
    return jax.shard_map(local, mesh=fine, in_specs=in_specs, out_specs=P("col", sec, None), check_vma=False)
```
